32 devices in a mesh: grp: 4 (over y, core), row: 4 (over z), col: 2 (over x).
Axes of the slice: x: 2, y: 2, z: 4, core: 2. Of those that a mesh axis runs over, the one named last changes fastest.
Arguments:
- field: float32 [8, 4, 512, 768], P(None, 'grp', 'row', 'col'), may hold values from -6 to 6
- previous: bfloat16 [8, 4, 512, 768], P(None, 'grp', 'row', 'col'), may hold values from -6 to 6
- kappa: float32 [4, 512, 768], P('grp', 'row', 'col'), may hold values from 0.02 to 0.1
- rates: float32 [8], replicated, may hold values from 0.5 to 1.6
- speeds: float32 [8, 3], replicated, may hold values from -0.5 to 0.5
- basis_x: bfloat16 [512, 128], replicated, may hold values from -0.25 to 0.25
- basis_y: bfloat16 [768, 128], replicated, may hold values from -0.21875 to 0.21875
Outputs:
- advanced: float32 [8, 4, 512, 768], P(None, 'grp', 'row', 'col')
- core: float32 [8, 4, 128, 128], P(None, 'grp')
- gram_x: float32 [512, 128], P('row')
- gram_y: float32 [768, 128], P(('col', 'row'))
The draws below stay inside these ranges and needn't reach their ends.
All inputs are finite; a program needn't handle non-finite values.
Results may differ from the reference program's by a relative error of at most 0.0029.
Values may be sent and summed in bfloat16 or wider, within the bound.
A program may use at most 64 MiB of HBM per device.

```python
import math
import jax
import jax.numpy as jnp
from jax import lax

SPECIES = 8
RANK = 128
NX = 512
NY = 768
NZ = 4


def levels(rng, dims, cuts, low, largest):
    gain = 1.0
    for position, shards_of in cuts:
        steps = jax.random.uniform(jax.random.fold_in(jax.random.fold_in(rng, 6), position), (shards_of,), jnp.float32, low / len(cuts), largest / len(cuts))
        gain = gain * jnp.repeat(jnp.exp(steps), dims[position] // shards_of).reshape((-1,) + (1,) * (len(dims) - 1 - position))
    return gain


def gaussian(rng, shape, scale, bound, pieces=(), kind=jnp.bfloat16):
    array = jax.random.normal(rng, shape, jnp.float32) * scale
    if len(pieces) > 0:
        array = levels(rng, shape, pieces, -0.22, 0.18) * array
    return jnp.clip(array, min=-bound, max=bound).astype(kind)


def setup_inputs(seed: int = 0) -> dict:
    splits = jax.random.split(jax.random.key(seed), 8)
    return {
        "field": gaussian(splits[0], (SPECIES, NZ, NX, NY), 1.0, 6.0, ((1, 4), (2, 4), (3, 2)), jnp.float32),
        "previous": gaussian(splits[1], (SPECIES, NZ, NX, NY), 1.0, 6.0, ((1, 4), (2, 4), (3, 2))),
        "kappa": jnp.clip(jnp.exp(math.log(0.1) - 1.609438 * jax.random.uniform(splits[2], (NZ, NX, NY), jnp.float32) ** levels(splits[2], (NZ, NX, NY), ((0, 4), (1, 4), (2, 2)), -0.2, 0.2)), 0.02, 0.1),
        "rates": jnp.clip(jnp.exp(jax.random.uniform(splits[3], (SPECIES,), jnp.float32, math.log(0.5), math.log(1.6))), 0.5, 1.6),
        "speeds": jnp.clip(jax.random.uniform(splits[4], (SPECIES, 3), jnp.float32, -0.5, 0.5), -0.5, 0.5),
        "basis_x": gaussian(splits[5], (NX, RANK), NX ** -0.5, 0.25),
        "basis_y": gaussian(splits[6], (NY, RANK), NY ** -0.5, 0.21875),
    }


def advance_species(packed):
    values, rate, speed, kappa = packed
    padded = jnp.pad(values, 1)
    z_next = padded[2:, 1:-1, 1:-1]
    z_prev = padded[:-2, 1:-1, 1:-1]
    x_next = padded[1:-1, 2:, 1:-1]
    x_prev = padded[1:-1, :-2, 1:-1]
    y_next = padded[1:-1, 1:-1, 2:]
    y_prev = padded[1:-1, 1:-1, :-2]
    laplace = z_next + z_prev + x_next + x_prev + y_next + y_prev - 6.0 * values
    transport = speed[0] * (z_next - z_prev) + speed[1] * (x_next - x_prev) + speed[2] * (y_next - y_prev)
    return values + kappa * rate * laplace - 0.5 * transport

def reference(field, previous, kappa, rates, speeds, basis_x, basis_y):
    high = lax.Precision.HIGHEST
    advanced = lax.map(lambda item: advance_species((item[0], item[1], item[2], kappa)), (field, rates, speeds))
    wide_x = basis_x.astype(jnp.float32)

    def project_species(slab):
        slab_wide = slab.astype(jnp.float32)
        projected = jnp.einsum('zxy,xr->zyr', slab_wide, wide_x, precision=high).astype(jnp.bfloat16)
        partial_x = jnp.einsum('zxy,zyr->xr', slab_wide, projected.astype(jnp.float32), precision=high)
        return (projected, partial_x)
    projected, partials = lax.map(project_species, previous)
    proj_wide = projected.astype(jnp.float32)
    core = jnp.einsum('szyr,yq->szrq', proj_wide, basis_y.astype(jnp.float32), precision=high)
    core_low = core.astype(jnp.bfloat16).astype(jnp.float32)
    scale_y = math.sqrt(NY) / (SPECIES * NZ * RANK)
    gram_y = scale_y * jnp.einsum('szyr,szrq->yq', proj_wide, core_low, precision=high)
    scale_x = math.sqrt(NX) / (SPECIES * NZ * NY)
    gram_x = scale_x * lax.optimization_barrier(jnp.sum(partials, axis=0))
    return (advanced, core, gram_x, gram_y)
```

```python
import functools
import math

import jax
import jax.numpy as jnp
from jax import lax
from jax.experimental import pallas as pl
from jax.experimental.pallas import tpu as pltpu
from jax.sharding import PartitionSpec as P

MESH = pl.DeviceIdType.MESH


def remote(src, dst, send, recv, target):
    return pltpu.make_async_remote_copy(
        src_ref=src,
        dst_ref=dst,
        send_sem=send,
        recv_sem=recv,
        device_id=target,
        device_id_type=MESH,
    )


def kernel(
    grp_n, row_n, col_n, scale_x, scale_y,
    field, prev, kappa, rates, speeds, basis_x, basis_y,
    advanced, core, gram_x, gram_y,
    field_v, kappa_v, bx_v, by_v, pair_v, q_v, proj_v, part_v, core_v,
    gx_acc, gx_in, gx_piece, gx_all, gy_acc, gy_in, gx_out, gy_out,
    z_out, z_in, x_out, x_in, y_out, y_in, adv_v,
    in_sem, own_sem, pair_s, pair_r, q_s, q_r, part_s, part_r, core_s, core_r, core_l,
    gx1_s, gx1_r, gx2_s, gx2_r, gy_s, gy_r, z_s, z_r, x_s, x_r, y_s, y_r, out_sem, fin_sem,
):
    species, width_x, width_y = field_v.shape
    half = species // 2
    pairs = row_n // 2
    rank = bx_v.shape[1]
    piece = width_x // grp_n
    part_y = width_y // row_n
    g = lax.axis_index("grp")
    r = lax.axis_index("row")
    c = lax.axis_index("col")
    a = r // 2
    b = r % 2
    team = 2 * grp_n
    ring = grp_n * col_n
    me_team = b * grp_n + g
    me_ring = c * grp_n + g

    def team_at(k):
        j = (me_team + k) % team
        return j, j // grp_n, j % grp_n

    def ring_at(k):
        j = (me_ring + k) % ring
        return j, j // grp_n, j % grp_n

    mine = [
        pltpu.make_async_copy(
            prev.at[b * half + i, 0],
            pair_v.at[i, pl.ds(pl.multiple_of(b * width_x, width_x), width_x)],
            own_sem.at[i],
        )
        for i in range(half)
    ]
    loads = [
        pltpu.make_async_copy(field.at[:, 0], field_v, in_sem.at[0]),
        pltpu.make_async_copy(kappa.at[0], kappa_v, in_sem.at[1]),
        pltpu.make_async_copy(
            basis_x.at[pl.ds(pl.multiple_of(a * 2 * width_x, 2 * width_x), 2 * width_x)],
            bx_v, in_sem.at[2],
        ),
        pltpu.make_async_copy(
            basis_y.at[pl.ds(pl.multiple_of(c * width_y, width_y), width_y)], by_v, in_sem.at[3]
        ),
    ]
    loads[0].start()
    for copy in mine:
        copy.start()
    for copy in loads[1:]:
        copy.start()

    barrier = pltpu.get_barrier_semaphore()
    count = 0
    for k in range(1, team):
        _, b_to, g_to = team_at(k)
        pl.semaphore_signal(
            barrier, inc=1, device_id={"grp": g_to, "row": 2 * a + b_to}, device_id_type=MESH
        )
        count += 1
    for d in range(1, col_n):
        for e in range(grp_n):
            pl.semaphore_signal(
                barrier, inc=1,
                device_id={"grp": (g + e) % grp_n, "col": (c + d) % col_n},
                device_id_type=MESH,
            )
            count += 1
    for d in range(1, pairs):
        pl.semaphore_signal(
            barrier, inc=1, device_id={"row": 2 * ((a + d) % pairs) + b}, device_id_type=MESH
        )
        count += 1

    @pl.when(r > 0)
    def _():
        pl.semaphore_signal(barrier, inc=1, device_id={"row": r - 1}, device_id_type=MESH)

    @pl.when(r < row_n - 1)
    def _():
        pl.semaphore_signal(barrier, inc=1, device_id={"row": r + 1}, device_id_type=MESH)

    neighbours = (r + row_n - 1) // row_n + (2 * row_n - 2 - r) // row_n
    pl.semaphore_wait(barrier, count + neighbours)

    def pair_copy(i, sender):
        return remote(
            prev.at[(1 - b) * half + i, 0],
            pair_v.at[i, pl.ds(pl.multiple_of(sender * width_x, width_x), width_x)],
            pair_s.at[i], pair_r.at[i], {"row": 2 * a + 1 - b},
        )

    for i in range(half):
        pair_copy(i, b).start()

    loads[0].wait()
    z_out[...] = field_v[...].astype(jnp.bfloat16)
    sides = (
        ("grp", g, grp_n, z_out, z_in, z_s, z_r),
        ("row", r, row_n, x_out, x_in, x_s, x_r),
        ("col", c, col_n, y_out, y_in, y_s, y_r),
    )

    def halo(axis, at, out, into, send, recv, up, shared):
        slot = 0 if up else 1
        return remote(
            out if shared else out.at[slot], into.at[slot], send.at[slot], recv.at[slot],
            {axis: at + 1 if up else at - 1},
        )

    def send_halos(k):
        axis, at, n, out, into, send, recv = sides[k]

        @pl.when(at < n - 1)
        def _():
            halo(axis, at, out, into, send, recv, True, k == 0).start()

        @pl.when(at > 0)
        def _():
            halo(axis, at, out, into, send, recv, False, k == 0).start()

    send_halos(0)
    lane = lax.broadcasted_iota(jnp.int32, (width_x, 128), 1)
    first = jnp.zeros((width_x, 128), jnp.float32)
    last = jnp.zeros((width_x, 128), jnp.float32)
    for s in range(species):
        x_out[0, s : s + 1, :] = field_v[s, width_x - 1 : width_x, :]
        x_out[1, s : s + 1, :] = field_v[s, 0:1, :]
        last = jnp.where(lane == s, field_v[s, :, width_y - 1 : width_y], last)
        first = jnp.where(lane == s, field_v[s, :, 0:1], first)
    y_out[0] = last
    y_out[1] = first
    send_halos(1)
    send_halos(2)

    def q_copy(i, d, sender, target):
        return remote(
            q_v.at[sender, i], q_v.at[sender, i], q_s.at[d, i], q_r.at[d, i],
            {"row": 2 * target + b},
        )

    loads[2].wait()
    for i in range(half):
        mine[i].wait()
        pair_copy(i, 1 - b).wait_recv()
        q_v[a, i] = lax.dot_general(
            bx_v[...], pair_v[i], (((0,), (0,)), ((), ())), preferred_element_type=jnp.float32
        ).astype(jnp.bfloat16)
        for d in range(1, pairs):
            q_copy(i, d, a, (a + d) % pairs).start()

    loads[1].wait()

    def receive_halos(k):
        axis, at, n, out, into, send, recv = sides[k]

        @pl.when(at > 0)
        def _():
            remote(
                out if k == 0 else out.at[0], into.at[0], send.at[0], recv.at[0], {axis: at - 1}
            ).wait_recv()

        @pl.when(at == 0)
        def _():
            into[0] = jnp.zeros(into.shape[1:], into.dtype)

        @pl.when(at < n - 1)
        def _():
            remote(
                out if k == 0 else out.at[1], into.at[1], send.at[1], recv.at[1], {axis: at + 1}
            ).wait_recv()

        @pl.when(at == n - 1)
        def _():
            into[1] = jnp.zeros(into.shape[1:], into.dtype)

    for k in (2, 1, 0):
        receive_halos(k)
    at_x = lax.broadcasted_iota(jnp.int32, (width_x, width_y), 0)
    at_y = lax.broadcasted_iota(jnp.int32, (width_x, width_y), 1)
    writes = []
    for s in range(species):
        u = field_v[s]
        z_prev = z_in[0, s].astype(jnp.float32)
        z_next = z_in[1, s].astype(jnp.float32)
        x_prev = jnp.where(at_x == 0, x_in[0, s : s + 1, :], pltpu.roll(u, 1, 0))
        x_next = jnp.where(at_x == width_x - 1, x_in[1, s : s + 1, :], pltpu.roll(u, width_x - 1, 0))
        y_prev = jnp.where(at_y == 0, y_in[0, :, s : s + 1], pltpu.roll(u, 1, 1))
        y_next = jnp.where(
            at_y == width_y - 1, y_in[1, :, s : s + 1], pltpu.roll(u, width_y - 1, 1)
        )
        laplace = z_next + z_prev + x_next + x_prev + y_next + y_prev - 6.0 * u
        transport = (
            speeds[s, 0] * (z_next - z_prev)
            + speeds[s, 1] * (x_next - x_prev)
            + speeds[s, 2] * (y_next - y_prev)
        )
        adv_v[s] = u + kappa_v[...] * rates[s] * laplace - 0.5 * transport
        copy = pltpu.make_async_copy(adv_v.at[s], advanced.at[s, 0], out_sem.at[s])
        copy.start()
        writes.append(copy)

    def part_copy(i, d, sender, target):
        return remote(
            part_v.at[sender, i], part_v.at[sender, i], part_s.at[d, i], part_r.at[d, i],
            {"col": target},
        )

    loads[3].wait()
    for i in range(half):
        for d in range(1, pairs):
            sender = (a + pairs - d) % pairs
            q_copy(i, d, sender, sender).wait_recv()
        total = q_v[0, i].astype(jnp.float32)
        for j in range(1, pairs):
            total = total + q_v[j, i].astype(jnp.float32)
        low = total.astype(jnp.bfloat16)
        proj_v[i] = low
        part_v[c, i] = jnp.dot(low, by_v[...], preferred_element_type=jnp.float32)
        for d in range(1, col_n):
            part_copy(i, d, c, (c + d) % col_n).start()
        product = lax.dot_general(
            pair_v[i], low, (((1,), (1,)), ((), ())), preferred_element_type=jnp.float32
        )
        gx_acc[...] = product if i == 0 else gx_acc[...] + product

    def gx1_copy(k, sender, target):
        j, b_to, g_to = target
        return remote(
            gx_acc.at[pl.ds(pl.multiple_of(j * piece, piece), piece)],
            gx_in.at[sender], gx1_s.at[k], gx1_r.at[k], {"grp": g_to, "row": 2 * a + b_to},
        )

    for k in range(1, team):
        gx1_copy(k, me_team, team_at(k)).start()
    gx_in[me_team] = gx_acc[pl.ds(pl.multiple_of(me_team * piece, piece), piece), :]

    def core_copy(i, owner):
        return remote(
            core_v.at[i], core.at[owner * half + i, 0], core_s.at[i], core_r.at[i],
            {"row": 2 * a + 1 - b},
        )

    core_writes = []
    for i in range(half):
        for d in range(1, col_n):
            sender = (c + col_n - d) % col_n
            part_copy(i, d, sender, sender).wait_recv()
        total = part_v[0, i]
        for j in range(1, col_n):
            total = total + part_v[j, i]
        core_v[i] = total
        core_copy(i, b).start()
        copy = pltpu.make_async_copy(core_v.at[i], core.at[b * half + i, 0], core_l.at[i])
        copy.start()
        core_writes.append(copy)
        product = lax.dot_general(
            proj_v[i], total.astype(jnp.bfloat16), (((0,), (0,)), ((), ())),
            preferred_element_type=jnp.float32,
        )
        gy_acc[...] = product if i == 0 else gy_acc[...] + product

    def gy_rows(b_to):
        return gy_acc.at[pl.ds(pl.multiple_of((2 * a + b_to) * part_y, part_y), part_y)]

    def gy_copy(k, sender, target):
        j, b_to, g_to = target
        return remote(
            gy_rows(b_to), gy_in.at[sender], gy_s.at[k], gy_r.at[k],
            {"grp": g_to, "row": 2 * a + b_to},
        )

    for k in range(1, team):
        gy_copy(k, me_team, team_at(k)).start()
    gy_in[me_team] = gy_acc[pl.ds(pl.multiple_of(r * part_y, part_y), part_y), :]

    for k in range(1, team):
        other = team_at(team - k)
        gx1_copy(k, other[0], other).wait_recv()
    total = gx_in[0]
    for j in range(1, team):
        total = total + gx_in[j]
    gx_piece[...] = total * scale_x

    def gx2_copy(k, sender, target):
        j, c_to, g_to = target
        return remote(
            gx_piece, gx_all.at[sender], gx2_s.at[k], gx2_r.at[k], {"grp": g_to, "col": c_to}
        )

    for k in range(1, ring):
        gx2_copy(k, me_ring, ring_at(k)).start()
    gx_all[me_ring] = gx_piece[...]

    for k in range(1, team):
        other = team_at(team - k)
        gy_copy(k, other[0], other).wait_recv()
    total = gy_in[0]
    for j in range(1, team):
        total = total + gy_in[j]
    gy_out[...] = total * scale_y
    gy_write = pltpu.make_async_copy(gy_out, gram_y, fin_sem.at[0])
    gy_write.start()

    for k in range(1, ring):
        other = ring_at(ring - k)
        gx2_copy(k, other[0], other).wait_recv()
    for e in range(grp_n):
        total = gx_all[e]
        for j in range(1, col_n):
            total = total + gx_all[j * grp_n + e]
        gx_out[e * piece : (e + 1) * piece, :] = total
    gx_write = pltpu.make_async_copy(gx_out, gram_x, fin_sem.at[1])
    gx_write.start()

    for i in range(half):
        core_copy(i, 1 - b).wait_recv()
        core_copy(i, b).wait_send()
        core_writes[i].wait()
        pair_copy(i, b).wait_send()
        for d in range(1, pairs):
            q_copy(i, d, a, (a + d) % pairs).wait_send()
        for d in range(1, col_n):
            part_copy(i, d, c, (c + d) % col_n).wait_send()
    for k in range(1, team):
        gx1_copy(k, me_team, team_at(k)).wait_send()
        gy_copy(k, me_team, team_at(k)).wait_send()
    for k in range(1, ring):
        gx2_copy(k, me_ring, ring_at(k)).wait_send()
    for k, (axis, at, n, out, into, send, recv) in enumerate(sides):

        @pl.when(at < n - 1)
        def _():
            halo(axis, at, out, into, send, recv, True, k == 0).wait_send()

        @pl.when(at > 0)
        def _():
            halo(axis, at, out, into, send, recv, False, k == 0).wait_send()

    for copy in writes:
        copy.wait()
    gy_write.wait()
    gx_write.wait()


def on_device(field, previous, kappa, rates, speeds, basis_x, basis_y):
    species, depth, width_x, width_y = field.shape
    rank = basis_x.shape[1]
    row_n = lax.axis_size("row")
    col_n = lax.axis_size("col")
    grp_n = lax.axis_size("grp")
    part_y = width_y // row_n
    grid_x = width_x * row_n
    grid_y = width_y * col_n
    grid_z = depth * grp_n
    scale_x = math.sqrt(grid_x) / (species * grid_z * grid_y)
    scale_y = math.sqrt(grid_y) / (species * grid_z * rank)
    half = species // 2
    pairs = row_n // 2
    piece = width_x // grp_n
    team = 2 * grp_n
    ring = grp_n * col_n
    f32, bf16 = jnp.float32, jnp.bfloat16
    dma = pltpu.SemaphoreType.DMA
    hbm = pl.BlockSpec(memory_space=pl.ANY)
    smem = pl.BlockSpec(memory_space=pltpu.SMEM)
    return pl.pallas_call(
        functools.partial(kernel, grp_n, row_n, col_n, scale_x, scale_y),
        out_shape=(
            jax.ShapeDtypeStruct(field.shape, f32),
            jax.ShapeDtypeStruct((species, depth, rank, rank), f32),
            jax.ShapeDtypeStruct((width_x, rank), f32),
            jax.ShapeDtypeStruct((part_y, rank), f32),
        ),
        in_specs=[hbm, hbm, hbm, smem, smem, hbm, hbm],
        out_specs=[hbm] * 4,
        scratch_shapes=[
            pltpu.VMEM((species, width_x, width_y), f32),
            pltpu.VMEM((width_x, width_y), f32),
            pltpu.VMEM((2 * width_x, rank), bf16),
            pltpu.VMEM((width_y, rank), bf16),
            pltpu.VMEM((half, 2 * width_x, width_y), bf16),
            pltpu.VMEM((pairs, half, rank, width_y), bf16),
            pltpu.VMEM((half, rank, width_y), bf16),
            pltpu.VMEM((col_n, half, rank, rank), f32),
            pltpu.VMEM((half, rank, rank), f32),
            pltpu.VMEM((2 * width_x, rank), f32),
            pltpu.VMEM((team, piece, rank), f32),
            pltpu.VMEM((piece, rank), f32),
            pltpu.VMEM((ring, piece, rank), f32),
            pltpu.VMEM((width_y, rank), f32),
            pltpu.VMEM((team, part_y, rank), f32),
            pltpu.VMEM((width_x, rank), f32),
            pltpu.VMEM((part_y, rank), f32),
            pltpu.VMEM((species, width_x, width_y), bf16),
            pltpu.VMEM((2, species, width_x, width_y), bf16),
            pltpu.VMEM((2, species, width_y), f32),
            pltpu.VMEM((2, species, width_y), f32),
            pltpu.VMEM((2, width_x, 128), f32),
            pltpu.VMEM((2, width_x, 128), f32),
            pltpu.VMEM((species, width_x, width_y), f32),
            dma((4,)), dma((half,)), dma((half,)), dma((half,)),
            dma((pairs, half)), dma((pairs, half)), dma((col_n, half)), dma((col_n, half)),
            dma((half,)), dma((half,)), dma((half,)),
            dma((team,)), dma((team,)), dma((ring,)), dma((ring,)), dma((team,)), dma((team,)),
            dma((2,)), dma((2,)), dma((2,)), dma((2,)), dma((2,)), dma((2,)),
            dma((species,)), dma((2,)),
        ],
        compiler_params=pltpu.CompilerParams(
            collective_id=0, has_side_effects=True, vmem_limit_bytes=40 * 1024 * 1024
        ),
    )(field, previous, kappa, rates, speeds, basis_x, basis_y)


def solution(mesh):
    return jax.shard_map(
        on_device,
        mesh=mesh,
        in_specs=(
            P(None, "grp", "row", "col"),
            P(None, "grp", "row", "col"),
            P("grp", "row", "col"),
            P(),
            P(),
            P(),
            P(),
        ),
        out_specs=(
            P(None, "grp", "row", "col"),
            P(None, "grp", None, None),
            P("row", None),
            P(("col", "row"), None),
        ),
        check_vma=False,
    )
```

```python
import functools
import math

import jax
import jax.numpy as jnp
from jax import lax
from jax.experimental import pallas as pl
from jax.experimental.pallas import tpu as pltpu
from jax.sharding import PartitionSpec as P

MESH = pl.DeviceIdType.MESH


def remote(src, dst, send, recv, target):
    return pltpu.make_async_remote_copy(
        src_ref=src,
        dst_ref=dst,
        send_sem=send,
        recv_sem=recv,
        device_id=target,
        device_id_type=MESH,
    )


def coded(value):
    square = value * value
    fourth = square * square
    return jnp.where(value < 0.0, -fourth, fourth).astype(jnp.bfloat16)


def decoded(code):
    wide = code.astype(jnp.float32)
    root = jnp.sqrt(jnp.sqrt(jnp.abs(wide)))
    return jnp.where(wide < 0.0, -root, root)


def kernel(
    grp_n, row_n, col_n, scale_x, scale_y,
    field, prev, kappa, rates, speeds, basis_x, basis_y,
    advanced, core, gram_x, gram_y,
    field_v, kappa_v, bx_v, by_v, pair_v, q_v, proj_v, part_v, core_v,
    gx_acc, gx_in, gx_piece, gx_all, gy_acc, gy_in, gx_out, gy_out,
    z_out, z_in, x_out, x_in, y_out, y_in, adv_v,
    in_sem, own_sem, pair_s, pair_r, q_s, q_r, part_s, part_r, core_s, core_r, core_l,
    gx1_s, gx1_r, gx2_s, gx2_r, gy_s, gy_r, z_s, z_r, x_s, x_r, y_s, y_r, out_sem, fin_sem,
):
    species, width_x, width_y = field_v.shape
    half = species // 2
    pairs = row_n // 2
    rank = bx_v.shape[1]
    piece = width_x // grp_n
    part_y = width_y // row_n
    g = lax.axis_index("grp")
    r = lax.axis_index("row")
    c = lax.axis_index("col")
    a = r // 2
    b = r % 2
    team = 2 * grp_n
    ring = grp_n * col_n
    me_team = b * grp_n + g
    me_ring = c * grp_n + g

    def team_at(k):
        j = (me_team + k) % team
        return j, j // grp_n, j % grp_n

    def ring_at(k):
        j = (me_ring + k) % ring
        return j, j // grp_n, j % grp_n

    mine = [
        pltpu.make_async_copy(
            prev.at[b * half + i, 0],
            pair_v.at[i, pl.ds(pl.multiple_of(b * width_x, width_x), width_x)],
            own_sem.at[i],
        )
        for i in range(half)
    ]
    loads = [
        pltpu.make_async_copy(field.at[:, 0], field_v, in_sem.at[0]),
        pltpu.make_async_copy(kappa.at[0], kappa_v, in_sem.at[1]),
        pltpu.make_async_copy(
            basis_x.at[pl.ds(pl.multiple_of(a * 2 * width_x, 2 * width_x), 2 * width_x)],
            bx_v, in_sem.at[2],
        ),
        pltpu.make_async_copy(
            basis_y.at[pl.ds(pl.multiple_of(c * width_y, width_y), width_y)], by_v, in_sem.at[3]
        ),
    ]
    loads[0].start()
    for copy in mine:
        copy.start()
    for copy in loads[1:]:
        copy.start()

    barrier = pltpu.get_barrier_semaphore()
    count = 0
    for k in range(1, team):
        _, b_to, g_to = team_at(k)
        pl.semaphore_signal(
            barrier, inc=1, device_id={"grp": g_to, "row": 2 * a + b_to}, device_id_type=MESH
        )
        count += 1
    for d in range(1, col_n):
        for e in range(grp_n):
            pl.semaphore_signal(
                barrier, inc=1,
                device_id={"grp": (g + e) % grp_n, "col": (c + d) % col_n},
                device_id_type=MESH,
            )
            count += 1
    for d in range(1, pairs):
        pl.semaphore_signal(
            barrier, inc=1, device_id={"row": 2 * ((a + d) % pairs) + b}, device_id_type=MESH
        )
        count += 1

    @pl.when(r > 0)
    def _():
        pl.semaphore_signal(barrier, inc=1, device_id={"row": r - 1}, device_id_type=MESH)

    @pl.when(r < row_n - 1)
    def _():
        pl.semaphore_signal(barrier, inc=1, device_id={"row": r + 1}, device_id_type=MESH)

    neighbours = (r + row_n - 1) // row_n + (2 * row_n - 2 - r) // row_n
    pl.semaphore_wait(barrier, count + neighbours)

    def pair_copy(i, sender):
        return remote(
            prev.at[(1 - b) * half + i, 0],
            pair_v.at[i, pl.ds(pl.multiple_of(sender * width_x, width_x), width_x)],
            pair_s.at[i], pair_r.at[i], {"row": 2 * a + 1 - b},
        )

    for i in range(half):
        pair_copy(i, b).start()

    loads[0].wait()
    z_out[...] = field_v[...].astype(jnp.bfloat16)
    sides = (
        ("grp", g, grp_n, z_out, z_in, z_s, z_r),
        ("row", r, row_n, x_out, x_in, x_s, x_r),
        ("col", c, col_n, y_out, y_in, y_s, y_r),
    )

    def halo(axis, at, out, into, send, recv, up, shared):
        slot = 0 if up else 1
        return remote(
            out if shared else out.at[slot], into.at[slot], send.at[slot], recv.at[slot],
            {axis: at + 1 if up else at - 1},
        )

    def send_halos(k):
        axis, at, n, out, into, send, recv = sides[k]

        @pl.when(at < n - 1)
        def _():
            halo(axis, at, out, into, send, recv, True, k == 0).start()

        @pl.when(at > 0)
        def _():
            halo(axis, at, out, into, send, recv, False, k == 0).start()

    send_halos(0)
    lane = lax.broadcasted_iota(jnp.int32, (width_x, 128), 1)
    first = jnp.zeros((width_x, 128), jnp.float32)
    last = jnp.zeros((width_x, 128), jnp.float32)
    for s in range(species):
        x_out[0, s : s + 1, :] = field_v[s, width_x - 1 : width_x, :]
        x_out[1, s : s + 1, :] = field_v[s, 0:1, :]
        last = jnp.where(lane == s, field_v[s, :, width_y - 1 : width_y], last)
        first = jnp.where(lane == s, field_v[s, :, 0:1], first)
    y_out[0] = last
    y_out[1] = first
    send_halos(1)
    send_halos(2)

    def q_copy(i, d, sender, target):
        return remote(
            q_v.at[sender, i], q_v.at[sender, i], q_s.at[d, i], q_r.at[d, i],
            {"row": 2 * target + b},
        )

    loads[2].wait()
    for i in range(half):
        mine[i].wait()
        pair_copy(i, 1 - b).wait_recv()
        q_v[a, i] = coded(
            lax.dot_general(
                bx_v[...], pair_v[i], (((0,), (0,)), ((), ())),
                preferred_element_type=jnp.float32,
            )
        )
        for d in range(1, pairs):
            q_copy(i, d, a, (a + d) % pairs).start()

    loads[1].wait()

    def receive_halos(k):
        axis, at, n, out, into, send, recv = sides[k]

        @pl.when(at > 0)
        def _():
            remote(
                out if k == 0 else out.at[0], into.at[0], send.at[0], recv.at[0], {axis: at - 1}
            ).wait_recv()

        @pl.when(at == 0)
        def _():
            into[0] = jnp.zeros(into.shape[1:], into.dtype)

        @pl.when(at < n - 1)
        def _():
            remote(
                out if k == 0 else out.at[1], into.at[1], send.at[1], recv.at[1], {axis: at + 1}
            ).wait_recv()

        @pl.when(at == n - 1)
        def _():
            into[1] = jnp.zeros(into.shape[1:], into.dtype)

    for k in (2, 1, 0):
        receive_halos(k)
    at_x = lax.broadcasted_iota(jnp.int32, (width_x, width_y), 0)
    at_y = lax.broadcasted_iota(jnp.int32, (width_x, width_y), 1)
    writes = []
    for s in range(species):
        u = field_v[s]
        z_prev = z_in[0, s].astype(jnp.float32)
        z_next = z_in[1, s].astype(jnp.float32)
        x_prev = jnp.where(at_x == 0, x_in[0, s : s + 1, :], pltpu.roll(u, 1, 0))
        x_next = jnp.where(at_x == width_x - 1, x_in[1, s : s + 1, :], pltpu.roll(u, width_x - 1, 0))
        y_prev = jnp.where(at_y == 0, y_in[0, :, s : s + 1], pltpu.roll(u, 1, 1))
        y_next = jnp.where(
            at_y == width_y - 1, y_in[1, :, s : s + 1], pltpu.roll(u, width_y - 1, 1)
        )
        laplace = z_next + z_prev + x_next + x_prev + y_next + y_prev - 6.0 * u
        transport = (
            speeds[0, s] * (z_next - z_prev)
            + speeds[1, s] * (x_next - x_prev)
            + speeds[2, s] * (y_next - y_prev)
        )
        adv_v[s] = u + kappa_v[...] * rates[s] * laplace - 0.5 * transport
        copy = pltpu.make_async_copy(adv_v.at[s], advanced.at[s, 0], out_sem.at[s])
        copy.start()
        writes.append(copy)

    def part_copy(i, d, sender, target):
        return remote(
            part_v.at[sender, i], part_v.at[sender, i], part_s.at[d, i], part_r.at[d, i],
            {"col": target},
        )

    loads[3].wait()
    for i in range(half):
        for d in range(1, pairs):
            sender = (a + pairs - d) % pairs
            q_copy(i, d, sender, sender).wait_recv()
        total = decoded(q_v[0, i])
        for j in range(1, pairs):
            total = total + decoded(q_v[j, i])
        low = total.astype(jnp.bfloat16)
        proj_v[i] = low
        part_v[c, i] = jnp.dot(low, by_v[...], preferred_element_type=jnp.float32)
        for d in range(1, col_n):
            part_copy(i, d, c, (c + d) % col_n).start()
        product = lax.dot_general(
            pair_v[i], low, (((1,), (1,)), ((), ())), preferred_element_type=jnp.float32
        )
        gx_acc[...] = product if i == 0 else gx_acc[...] + product

    def gx1_copy(k, sender, target):
        j, b_to, g_to = target
        return remote(
            gx_acc.at[pl.ds(pl.multiple_of(j * piece, piece), piece)],
            gx_in.at[sender], gx1_s.at[k], gx1_r.at[k], {"grp": g_to, "row": 2 * a + b_to},
        )

    for k in range(1, team):
        gx1_copy(k, me_team, team_at(k)).start()
    gx_in[me_team] = gx_acc[pl.ds(pl.multiple_of(me_team * piece, piece), piece), :]

    def core_copy(i, owner):
        return remote(
            core_v.at[i], core.at[owner * half + i, 0], core_s.at[i], core_r.at[i],
            {"row": 2 * a + 1 - b},
        )

    core_writes = []
    for i in range(half):
        for d in range(1, col_n):
            sender = (c + col_n - d) % col_n
            part_copy(i, d, sender, sender).wait_recv()
        total = part_v[0, i]
        for j in range(1, col_n):
            total = total + part_v[j, i]
        core_v[i] = total
        core_copy(i, b).start()
        copy = pltpu.make_async_copy(core_v.at[i], core.at[b * half + i, 0], core_l.at[i])
        copy.start()
        core_writes.append(copy)
        product = lax.dot_general(
            proj_v[i], total.astype(jnp.bfloat16), (((0,), (0,)), ((), ())),
            preferred_element_type=jnp.float32,
        )
        gy_acc[...] = product if i == 0 else gy_acc[...] + product

    def gy_rows(b_to):
        return gy_acc.at[pl.ds(pl.multiple_of((2 * a + b_to) * part_y, part_y), part_y)]

    def gy_copy(k, sender, target):
        j, b_to, g_to = target
        return remote(
            gy_rows(b_to), gy_in.at[sender], gy_s.at[k], gy_r.at[k],
            {"grp": g_to, "row": 2 * a + b_to},
        )

    for k in range(1, team):
        gy_copy(k, me_team, team_at(k)).start()
    gy_in[me_team] = gy_acc[pl.ds(pl.multiple_of(r * part_y, part_y), part_y), :]

    for k in range(1, team):
        other = team_at(team - k)
        gx1_copy(k, other[0], other).wait_recv()
    total = gx_in[0]
    for j in range(1, team):
        total = total + gx_in[j]
    gx_piece[...] = total * scale_x

    def gx2_copy(k, sender, target):
        j, c_to, g_to = target
        return remote(
            gx_piece, gx_all.at[sender], gx2_s.at[k], gx2_r.at[k], {"grp": g_to, "col": c_to}
        )

    for k in range(1, ring):
        gx2_copy(k, me_ring, ring_at(k)).start()
    gx_all[me_ring] = gx_piece[...]

    for k in range(1, team):
        other = team_at(team - k)
        gy_copy(k, other[0], other).wait_recv()
    total = gy_in[0]
    for j in range(1, team):
        total = total + gy_in[j]
    gy_out[...] = total * scale_y
    gy_write = pltpu.make_async_copy(gy_out, gram_y, fin_sem.at[0])
    gy_write.start()

    for k in range(1, ring):
        other = ring_at(ring - k)
        gx2_copy(k, other[0], other).wait_recv()
    for e in range(grp_n):
        total = gx_all[e]
        for j in range(1, col_n):
            total = total + gx_all[j * grp_n + e]
        gx_out[e * piece : (e + 1) * piece, :] = total
    gx_write = pltpu.make_async_copy(gx_out, gram_x, fin_sem.at[1])
    gx_write.start()

    for i in range(half):
        core_copy(i, 1 - b).wait_recv()
        core_copy(i, b).wait_send()
        core_writes[i].wait()
        pair_copy(i, b).wait_send()
        for d in range(1, pairs):
            q_copy(i, d, a, (a + d) % pairs).wait_send()
        for d in range(1, col_n):
            part_copy(i, d, c, (c + d) % col_n).wait_send()
    for k in range(1, team):
        gx1_copy(k, me_team, team_at(k)).wait_send()
        gy_copy(k, me_team, team_at(k)).wait_send()
    for k in range(1, ring):
        gx2_copy(k, me_ring, ring_at(k)).wait_send()
    for k, (axis, at, n, out, into, send, recv) in enumerate(sides):

        @pl.when(at < n - 1)
        def _():
            halo(axis, at, out, into, send, recv, True, k == 0).wait_send()

        @pl.when(at > 0)
        def _():
            halo(axis, at, out, into, send, recv, False, k == 0).wait_send()

    for copy in writes:
        copy.wait()
    gy_write.wait()
    gx_write.wait()


def on_device(field, previous, kappa, rates, speeds, basis_x, basis_y):
    species, depth, width_x, width_y = field.shape
    rank = basis_x.shape[1]
    row_n = lax.axis_size("row")
    col_n = lax.axis_size("col")
    grp_n = lax.axis_size("grp")
    part_y = width_y // row_n
    grid_x = width_x * row_n
    grid_y = width_y * col_n
    grid_z = depth * grp_n
    scale_x = math.sqrt(grid_x) / (species * grid_z * grid_y)
    scale_y = math.sqrt(grid_y) / (species * grid_z * rank)
    half = species // 2
    pairs = row_n // 2
    piece = width_x // grp_n
    team = 2 * grp_n
    ring = grp_n * col_n
    f32, bf16 = jnp.float32, jnp.bfloat16
    dma = pltpu.SemaphoreType.DMA
    hbm = pl.BlockSpec(memory_space=pl.ANY)
    smem = pl.BlockSpec(memory_space=pltpu.SMEM)
    return pl.pallas_call(
        functools.partial(kernel, grp_n, row_n, col_n, scale_x, scale_y),
        out_shape=(
            jax.ShapeDtypeStruct(field.shape, f32),
            jax.ShapeDtypeStruct((species, depth, rank, rank), f32),
            jax.ShapeDtypeStruct((width_x, rank), f32),
            jax.ShapeDtypeStruct((part_y, rank), f32),
        ),
        in_specs=[hbm, hbm, hbm, smem, smem, hbm, hbm],
        out_specs=[hbm] * 4,
        scratch_shapes=[
            pltpu.VMEM((species, width_x, width_y), f32),
            pltpu.VMEM((width_x, width_y), f32),
            pltpu.VMEM((2 * width_x, rank), bf16),
            pltpu.VMEM((width_y, rank), bf16),
            pltpu.VMEM((half, 2 * width_x, width_y), bf16),
            pltpu.VMEM((pairs, half, rank, width_y), bf16),
            pltpu.VMEM((half, rank, width_y), bf16),
            pltpu.VMEM((col_n, half, rank, rank), f32),
            pltpu.VMEM((half, rank, rank), f32),
            pltpu.VMEM((2 * width_x, rank), f32),
            pltpu.VMEM((team, piece, rank), f32),
            pltpu.VMEM((piece, rank), f32),
            pltpu.VMEM((ring, piece, rank), f32),
            pltpu.VMEM((width_y, rank), f32),
            pltpu.VMEM((team, part_y, rank), f32),
            pltpu.VMEM((width_x, rank), f32),
            pltpu.VMEM((part_y, rank), f32),
            pltpu.VMEM((species, width_x, width_y), bf16),
            pltpu.VMEM((2, species, width_x, width_y), bf16),
            pltpu.VMEM((2, species, width_y), f32),
            pltpu.VMEM((2, species, width_y), f32),
            pltpu.VMEM((2, width_x, 128), f32),
            pltpu.VMEM((2, width_x, 128), f32),
            pltpu.VMEM((species, width_x, width_y), f32),
            dma((4,)), dma((half,)), dma((half,)), dma((half,)),
            dma((pairs, half)), dma((pairs, half)), dma((col_n, half)), dma((col_n, half)),
            dma((half,)), dma((half,)), dma((half,)),
            dma((team,)), dma((team,)), dma((ring,)), dma((ring,)), dma((team,)), dma((team,)),
            dma((2,)), dma((2,)), dma((2,)), dma((2,)), dma((2,)), dma((2,)),
            dma((species,)), dma((2,)),
        ],
        compiler_params=pltpu.CompilerParams(
            collective_id=0, has_side_effects=True, vmem_limit_bytes=60 * 1024 * 1024
        ),
    )(field, previous, kappa, rates, speeds.T, basis_x, basis_y)


def solution(mesh):
    return jax.shard_map(
        on_device,
        mesh=mesh,
        in_specs=(
            P(None, "grp", "row", "col"),
            P(None, "grp", "row", "col"),
            P("grp", "row", "col"),
            P(),
            P(),
            P(),
            P(),
        ),
        out_specs=(
            P(None, "grp", "row", "col"),
            P(None, "grp", None, None),
            P("row", None),
            P(("col", "row"), None),
        ),
        check_vma=False,
    )
```

```python
import functools
import math

import jax
import jax.numpy as jnp
from jax import lax
from jax.experimental import pallas as pl
from jax.experimental.pallas import tpu as pltpu
from jax.sharding import PartitionSpec as P

MESH = pl.DeviceIdType.MESH


def remote(src, dst, send, recv, target):
    return pltpu.make_async_remote_copy(
        src_ref=src,
        dst_ref=dst,
        send_sem=send,
        recv_sem=recv,
        device_id=target,
        device_id_type=MESH,
    )


def coded(value):
    square = value * value
    fourth = square * square
    return jnp.where(value < 0.0, -fourth, fourth).astype(jnp.bfloat16)


def decoded(code):
    wide = code.astype(jnp.float32)
    root = jnp.sqrt(jnp.sqrt(jnp.abs(wide)))
    return jnp.where(wide < 0.0, -root, root)


def squared(value):
    square = value * value
    return jnp.where(value < 0.0, -square, square).astype(jnp.bfloat16)


def rooted(code):
    wide = code.astype(jnp.float32)
    root = jnp.sqrt(jnp.abs(wide))
    return jnp.where(wide < 0.0, -root, root)


def kernel(
    grp_n, row_n, col_n, scale_x, scale_y,
    field, prev, kappa, rates, speeds, basis_x, basis_y,
    advanced, core, gram_x, gram_y,
    field_v, kappa_v, bx_v, by_v, pair_v, q_v, proj_v, part_v, core_v, core_out, core_in,
    gx_acc, gx_code, gx_in, gx_piece, gx_all, gy_acc, gy_code, gy_in, gx_out, gy_out,
    z_out, z_in, x_out, x_in, y_out, y_in, adv_v,
    in_sem, own_sem, pair_s, pair_r, q_s, q_r, part_s, part_r, core_s, core_r, core_l,
    gx1_s, gx1_r, gx2_s, gx2_r, gy_s, gy_r, z_s, z_r, x_s, x_r, y_s, y_r, out_sem, fin_sem,
):
    species, width_x, width_y = field_v.shape
    half = species // 2
    pairs = row_n // 2
    rank = bx_v.shape[1]
    piece = width_x // grp_n
    part_y = width_y // row_n
    g = lax.axis_index("grp")
    r = lax.axis_index("row")
    c = lax.axis_index("col")
    a = r // 2
    b = r % 2
    team = 2 * grp_n
    ring = grp_n * col_n
    me_team = b * grp_n + g
    me_ring = c * grp_n + g

    def team_at(k):
        j = (me_team + k) % team
        return j, j // grp_n, j % grp_n

    def ring_at(k):
        j = (me_ring + k) % ring
        return j, j // grp_n, j % grp_n

    mine = [
        pltpu.make_async_copy(
            prev.at[b * half + i, 0],
            pair_v.at[i, pl.ds(pl.multiple_of(b * width_x, width_x), width_x)],
            own_sem.at[i],
        )
        for i in range(half)
    ]
    loads = [
        pltpu.make_async_copy(field.at[:, 0], field_v, in_sem.at[0]),
        pltpu.make_async_copy(kappa.at[0], kappa_v, in_sem.at[1]),
        pltpu.make_async_copy(
            basis_x.at[pl.ds(pl.multiple_of(a * 2 * width_x, 2 * width_x), 2 * width_x)],
            bx_v, in_sem.at[2],
        ),
        pltpu.make_async_copy(
            basis_y.at[pl.ds(pl.multiple_of(c * width_y, width_y), width_y)], by_v, in_sem.at[3]
        ),
    ]
    loads[0].start()
    for copy in mine:
        copy.start()
    for copy in loads[1:]:
        copy.start()

    barrier = pltpu.get_barrier_semaphore()
    count = 0
    for k in range(1, team):
        _, b_to, g_to = team_at(k)
        pl.semaphore_signal(
            barrier, inc=1, device_id={"grp": g_to, "row": 2 * a + b_to}, device_id_type=MESH
        )
        count += 1
    for d in range(1, col_n):
        for e in range(grp_n):
            pl.semaphore_signal(
                barrier, inc=1,
                device_id={"grp": (g + e) % grp_n, "col": (c + d) % col_n},
                device_id_type=MESH,
            )
            count += 1
    for d in range(1, pairs):
        pl.semaphore_signal(
            barrier, inc=1, device_id={"row": 2 * ((a + d) % pairs) + b}, device_id_type=MESH
        )
        count += 1

    @pl.when(r > 0)
    def _():
        pl.semaphore_signal(barrier, inc=1, device_id={"row": r - 1}, device_id_type=MESH)

    @pl.when(r < row_n - 1)
    def _():
        pl.semaphore_signal(barrier, inc=1, device_id={"row": r + 1}, device_id_type=MESH)

    neighbours = (r + row_n - 1) // row_n + (2 * row_n - 2 - r) // row_n
    pl.semaphore_wait(barrier, count + neighbours)

    def pair_copy(i, sender):
        return remote(
            prev.at[(1 - b) * half + i, 0],
            pair_v.at[i, pl.ds(pl.multiple_of(sender * width_x, width_x), width_x)],
            pair_s.at[i], pair_r.at[i], {"row": 2 * a + 1 - b},
        )

    for i in range(half):
        pair_copy(i, b).start()

    loads[0].wait()
    z_out[...] = field_v[...].astype(jnp.bfloat16)
    sides = (
        ("grp", g, grp_n, z_out, z_in, z_s, z_r),
        ("row", r, row_n, x_out, x_in, x_s, x_r),
        ("col", c, col_n, y_out, y_in, y_s, y_r),
    )

    def halo(axis, at, out, into, send, recv, up, shared):
        slot = 0 if up else 1
        return remote(
            out if shared else out.at[slot], into.at[slot], send.at[slot], recv.at[slot],
            {axis: at + 1 if up else at - 1},
        )

    def send_halos(k):
        axis, at, n, out, into, send, recv = sides[k]

        @pl.when(at < n - 1)
        def _():
            halo(axis, at, out, into, send, recv, True, k == 0).start()

        @pl.when(at > 0)
        def _():
            halo(axis, at, out, into, send, recv, False, k == 0).start()

    send_halos(0)
    lane = lax.broadcasted_iota(jnp.int32, (width_x, 128), 1)
    first = jnp.zeros((width_x, 128), jnp.float32)
    last = jnp.zeros((width_x, 128), jnp.float32)
    for s in range(species):
        x_out[0, s : s + 1, :] = field_v[s, width_x - 1 : width_x, :]
        x_out[1, s : s + 1, :] = field_v[s, 0:1, :]
        last = jnp.where(lane == s, field_v[s, :, width_y - 1 : width_y], last)
        first = jnp.where(lane == s, field_v[s, :, 0:1], first)
    y_out[0] = last
    y_out[1] = first
    send_halos(1)
    send_halos(2)

    def q_copy(i, d, sender, target):
        return remote(
            q_v.at[sender, i], q_v.at[sender, i], q_s.at[d, i], q_r.at[d, i],
            {"row": 2 * target + b},
        )

    loads[2].wait()
    for i in range(half):
        mine[i].wait()
        pair_copy(i, 1 - b).wait_recv()
        q_v[a, i] = coded(
            lax.dot_general(
                bx_v[...], pair_v[i], (((0,), (0,)), ((), ())),
                preferred_element_type=jnp.float32,
            )
        )
        for d in range(1, pairs):
            q_copy(i, d, a, (a + d) % pairs).start()

    loads[1].wait()

    def receive_halos(k):
        axis, at, n, out, into, send, recv = sides[k]

        @pl.when(at > 0)
        def _():
            remote(
                out if k == 0 else out.at[0], into.at[0], send.at[0], recv.at[0], {axis: at - 1}
            ).wait_recv()

        @pl.when(at == 0)
        def _():
            into[0] = jnp.zeros(into.shape[1:], into.dtype)

        @pl.when(at < n - 1)
        def _():
            remote(
                out if k == 0 else out.at[1], into.at[1], send.at[1], recv.at[1], {axis: at + 1}
            ).wait_recv()

        @pl.when(at == n - 1)
        def _():
            into[1] = jnp.zeros(into.shape[1:], into.dtype)

    for k in (2, 1, 0):
        receive_halos(k)
    at_x = lax.broadcasted_iota(jnp.int32, (width_x, width_y), 0)
    at_y = lax.broadcasted_iota(jnp.int32, (width_x, width_y), 1)
    writes = []
    for s in range(species):
        u = field_v[s]
        z_prev = z_in[0, s].astype(jnp.float32)
        z_next = z_in[1, s].astype(jnp.float32)
        x_prev = jnp.where(at_x == 0, x_in[0, s : s + 1, :], pltpu.roll(u, 1, 0))
        x_next = jnp.where(at_x == width_x - 1, x_in[1, s : s + 1, :], pltpu.roll(u, width_x - 1, 0))
        y_prev = jnp.where(at_y == 0, y_in[0, :, s : s + 1], pltpu.roll(u, 1, 1))
        y_next = jnp.where(
            at_y == width_y - 1, y_in[1, :, s : s + 1], pltpu.roll(u, width_y - 1, 1)
        )
        laplace = z_next + z_prev + x_next + x_prev + y_next + y_prev - 6.0 * u
        transport = (
            speeds[0, s] * (z_next - z_prev)
            + speeds[1, s] * (x_next - x_prev)
            + speeds[2, s] * (y_next - y_prev)
        )
        adv_v[s] = u + kappa_v[...] * rates[s] * laplace - 0.5 * transport
        copy = pltpu.make_async_copy(adv_v.at[s], advanced.at[s, 0], out_sem.at[s])
        copy.start()
        writes.append(copy)

    def part_copy(i, d, sender, target):
        return remote(
            part_v.at[sender, i], part_v.at[sender, i], part_s.at[d, i], part_r.at[d, i],
            {"col": target},
        )

    def core_copy(i):
        return remote(
            core_out.at[i], core_in.at[i], core_s.at[i], core_r.at[i], {"row": 2 * a + 1 - b}
        )

    def core_write(i, owner, at):
        return pltpu.make_async_copy(
            core_v.at[at, i], core.at[owner * half + i, 0], core_l.at[at, i]
        )

    def finish_core(i):
        for d in range(1, col_n):
            sender = (c + col_n - d) % col_n
            part_copy(i, d, sender, sender).wait_recv()
        total = part_v[0, i]
        for j in range(1, col_n):
            total = total + part_v[j, i]
        code = coded(total)
        core_out[i] = code
        core_copy(i).start()
        product = lax.dot_general(
            proj_v[i], total.astype(jnp.bfloat16), (((0,), (0,)), ((), ())),
            preferred_element_type=jnp.float32,
        )
        gy_acc[...] = product if i == 0 else gy_acc[...] + product

    loads[3].wait()
    for i in range(half):
        for d in range(1, pairs):
            sender = (a + pairs - d) % pairs
            q_copy(i, d, sender, sender).wait_recv()
        total = decoded(q_v[0, i])
        for j in range(1, pairs):
            total = total + decoded(q_v[j, i])
        low = total.astype(jnp.bfloat16)
        proj_v[i] = low
        part_v[c, i] = jnp.dot(low, by_v[...], preferred_element_type=jnp.float32)
        for d in range(1, col_n):
            part_copy(i, d, c, (c + d) % col_n).start()
        product = lax.dot_general(
            pair_v[i], low, (((1,), (1,)), ((), ())), preferred_element_type=jnp.float32
        )
        gx_acc[...] = product if i == 0 else gx_acc[...] + product
        if 0 < i < half - 1:
            finish_core(i - 1)

    def gx1_copy(k, sender, target):
        j, b_to, g_to = target
        return remote(
            gx_code.at[pl.ds(pl.multiple_of(j * piece, piece), piece)],
            gx_in.at[sender], gx1_s.at[k], gx1_r.at[k], {"grp": g_to, "row": 2 * a + b_to},
        )

    gx_code[...] = squared(gx_acc[...])
    for k in range(1, team):
        gx1_copy(k, me_team, team_at(k)).start()
    gx_in[me_team] = gx_code[pl.ds(pl.multiple_of(me_team * piece, piece), piece), :]
    for i in range(max(half - 2, 0), half):
        finish_core(i)

    def gy_rows(b_to):
        return gy_code.at[pl.ds(pl.multiple_of((2 * a + b_to) * part_y, part_y), part_y)]

    def gy_copy(k, sender, target):
        j, b_to, g_to = target
        return remote(
            gy_rows(b_to), gy_in.at[sender], gy_s.at[k], gy_r.at[k],
            {"grp": g_to, "row": 2 * a + b_to},
        )

    gy_code[...] = squared(gy_acc[...])
    for k in range(1, team):
        gy_copy(k, me_team, team_at(k)).start()
    gy_in[me_team] = gy_code[pl.ds(pl.multiple_of(r * part_y, part_y), part_y), :]

    for k in range(1, team):
        other = team_at(team - k)
        gx1_copy(k, other[0], other).wait_recv()
    total = rooted(gx_in[0])
    for j in range(1, team):
        total = total + rooted(gx_in[j])
    gx_piece[...] = total * scale_x

    def gx2_copy(k, sender, target):
        j, c_to, g_to = target
        return remote(
            gx_piece, gx_all.at[sender], gx2_s.at[k], gx2_r.at[k], {"grp": g_to, "col": c_to}
        )

    for k in range(1, ring):
        gx2_copy(k, me_ring, ring_at(k)).start()
    gx_all[me_ring] = gx_piece[...]

    for i in range(half):
        core_v[0, i] = decoded(core_out[i])
        core_write(i, b, 0).start()
        core_copy(i).wait_recv()
        core_v[1, i] = decoded(core_in[i])
        core_write(i, 1 - b, 1).start()

    for k in range(1, team):
        other = team_at(team - k)
        gy_copy(k, other[0], other).wait_recv()
    total = rooted(gy_in[0])
    for j in range(1, team):
        total = total + rooted(gy_in[j])
    gy_out[...] = total * scale_y
    gy_write = pltpu.make_async_copy(gy_out, gram_y, fin_sem.at[0])
    gy_write.start()

    for k in range(1, ring):
        other = ring_at(ring - k)
        gx2_copy(k, other[0], other).wait_recv()
    for e in range(grp_n):
        total = gx_all[e]
        for j in range(1, col_n):
            total = total + gx_all[j * grp_n + e]
        gx_out[e * piece : (e + 1) * piece, :] = total
    gx_write = pltpu.make_async_copy(gx_out, gram_x, fin_sem.at[1])
    gx_write.start()

    for i in range(half):
        core_copy(i).wait_send()
        core_write(i, b, 0).wait()
        core_write(i, 1 - b, 1).wait()
        pair_copy(i, b).wait_send()
        for d in range(1, pairs):
            q_copy(i, d, a, (a + d) % pairs).wait_send()
        for d in range(1, col_n):
            part_copy(i, d, c, (c + d) % col_n).wait_send()
    for k in range(1, team):
        gx1_copy(k, me_team, team_at(k)).wait_send()
        gy_copy(k, me_team, team_at(k)).wait_send()
    for k in range(1, ring):
        gx2_copy(k, me_ring, ring_at(k)).wait_send()
    for k, (axis, at, n, out, into, send, recv) in enumerate(sides):

        @pl.when(at < n - 1)
        def _():
            halo(axis, at, out, into, send, recv, True, k == 0).wait_send()

        @pl.when(at > 0)
        def _():
            halo(axis, at, out, into, send, recv, False, k == 0).wait_send()

    for copy in writes:
        copy.wait()
    gy_write.wait()
    gx_write.wait()


def on_device(field, previous, kappa, rates, speeds, basis_x, basis_y):
    species, depth, width_x, width_y = field.shape
    rank = basis_x.shape[1]
    row_n = lax.axis_size("row")
    col_n = lax.axis_size("col")
    grp_n = lax.axis_size("grp")
    part_y = width_y // row_n
    grid_x = width_x * row_n
    grid_y = width_y * col_n
    grid_z = depth * grp_n
    scale_x = math.sqrt(grid_x) / (species * grid_z * grid_y)
    scale_y = math.sqrt(grid_y) / (species * grid_z * rank)
    half = species // 2
    pairs = row_n // 2
    piece = width_x // grp_n
    team = 2 * grp_n
    ring = grp_n * col_n
    f32, bf16 = jnp.float32, jnp.bfloat16
    dma = pltpu.SemaphoreType.DMA
    hbm = pl.BlockSpec(memory_space=pl.ANY)
    smem = pl.BlockSpec(memory_space=pltpu.SMEM)
    return pl.pallas_call(
        functools.partial(kernel, grp_n, row_n, col_n, scale_x, scale_y),
        out_shape=(
            jax.ShapeDtypeStruct(field.shape, f32),
            jax.ShapeDtypeStruct((species, depth, rank, rank), f32),
            jax.ShapeDtypeStruct((width_x, rank), f32),
            jax.ShapeDtypeStruct((part_y, rank), f32),
        ),
        in_specs=[hbm, hbm, hbm, smem, smem, hbm, hbm],
        out_specs=[hbm] * 4,
        scratch_shapes=[
            pltpu.VMEM((species, width_x, width_y), f32),
            pltpu.VMEM((width_x, width_y), f32),
            pltpu.VMEM((2 * width_x, rank), bf16),
            pltpu.VMEM((width_y, rank), bf16),
            pltpu.VMEM((half, 2 * width_x, width_y), bf16),
            pltpu.VMEM((pairs, half, rank, width_y), bf16),
            pltpu.VMEM((half, rank, width_y), bf16),
            pltpu.VMEM((col_n, half, rank, rank), f32),
            pltpu.VMEM((2, half, rank, rank), f32),
            pltpu.VMEM((half, rank, rank), bf16),
            pltpu.VMEM((half, rank, rank), bf16),
            pltpu.VMEM((2 * width_x, rank), f32),
            pltpu.VMEM((2 * width_x, rank), bf16),
            pltpu.VMEM((team, piece, rank), bf16),
            pltpu.VMEM((piece, rank), f32),
            pltpu.VMEM((ring, piece, rank), f32),
            pltpu.VMEM((width_y, rank), f32),
            pltpu.VMEM((width_y, rank), bf16),
            pltpu.VMEM((team, part_y, rank), bf16),
            pltpu.VMEM((width_x, rank), f32),
            pltpu.VMEM((part_y, rank), f32),
            pltpu.VMEM((species, width_x, width_y), bf16),
            pltpu.VMEM((2, species, width_x, width_y), bf16),
            pltpu.VMEM((2, species, width_y), f32),
            pltpu.VMEM((2, species, width_y), f32),
            pltpu.VMEM((2, width_x, 128), f32),
            pltpu.VMEM((2, width_x, 128), f32),
            pltpu.VMEM((species, width_x, width_y), f32),
            dma((4,)), dma((half,)), dma((half,)), dma((half,)),
            dma((pairs, half)), dma((pairs, half)), dma((col_n, half)), dma((col_n, half)),
            dma((half,)), dma((half,)), dma((2, half)),
            dma((team,)), dma((team,)), dma((ring,)), dma((ring,)), dma((team,)), dma((team,)),
            dma((2,)), dma((2,)), dma((2,)), dma((2,)), dma((2,)), dma((2,)),
            dma((species,)), dma((2,)),
        ],
        compiler_params=pltpu.CompilerParams(
            collective_id=0, has_side_effects=True, vmem_limit_bytes=60 * 1024 * 1024
        ),
    )(field, previous, kappa, rates, speeds.T, basis_x, basis_y)


def solution(mesh):
    return jax.shard_map(
        on_device,
        mesh=mesh,
        in_specs=(
            P(None, "grp", "row", "col"),
            P(None, "grp", "row", "col"),
            P("grp", "row", "col"),
            P(),
            P(),
            P(),
            P(),
        ),
        out_specs=(
            P(None, "grp", "row", "col"),
            P(None, "grp", None, None),
            P("row", None),
            P(("col", "row"), None),
        ),
        check_vma=False,
    )
```
